512 devices in a mesh: sub: 64 (over x, y, core), sep: 8 (over z).
Axes of the slice: x: 4, y: 8, z: 8, core: 2. Of those that a mesh axis runs over, the one named last changes fastest.
Arguments:
- sep_in: float32 [64, 4, 8, 32768], P('sub', None, None, 'sep'), may hold values from -6 to 6
- inv_blocks: bfloat16 [64, 64, 64, 1024], P('sub', None, None, 'sep'), may hold values from -0.75 to 0.75
- couple_blocks: bfloat16 [64, 2, 64, 64, 1024], P('sub', None, None, None, 'sep'), may hold values from -0.5 to 0.5
- face_index: int32 [64, 2, 1024], P('sub', None, 'sep'), may hold values from 0 to 4095
- sep_diag: float32 [64, 32, 32768], P('sub', 'sep'), may hold values from 1 to 3
- sep_couple: float32 [4, 2, 64, 64], replicated, may hold values from -0.5 to 0.5
- sep_index: int32 [64, 32, 512, 2], P('sub', 'sep'), may hold values from 0 to 511
Outputs:
- schur_image: float32 [64, 32, 32768], P('sub', 'sep')
The draws below stay inside these ranges and needn't reach their ends.
All inputs are finite; a program needn't handle non-finite values.
Results may differ from the reference program's by a relative error of at most 0.0015.
Values may be sent and summed in bfloat16 or wider, within the bound.
A program may use at most 64 MiB of HBM per device.

```python
import jax
import jax.numpy as jnp
from jax import lax

BS = 64
LEV = 4
KI = 2
KS = 2
HC = 8
ZB = 64
NB = 128
ROWS = 32
FBD = 4096
NZ = 32768
NZB = 512
NBT = 1024
N_SUB = 64
N_SEP = 8


def plant(values, own_key, smallest, largest):
    longest = values.shape.index(max(values.shape))
    spots = []
    for shift in (0, 1):
        where = [jax.random.randint(jax.random.fold_in(own_key, axis), (), 0, length) for axis, length in enumerate(values.shape)]
        where[longest] = (where[longest] + shift) % values.shape[longest]
        spots.append(tuple(where))
    return values.at[spots[0]].set(smallest).at[spots[1]].set(largest)


def block_levels(key, extent, shards, least, largest):
    gain = 1.0
    for axis_at, blocks in shards:
        heights = jax.random.uniform(jax.random.fold_in(jax.random.fold_in(key, 6), axis_at), (blocks,), jnp.float32, least / len(shards), largest / len(shards))
        gain = gain * jnp.repeat(jnp.exp(heights), extent[axis_at] // blocks).reshape((-1,) + (1,) * (len(extent) - 1 - axis_at))
    return gain


def scatter_about(rng, shape, scale, bound, shards=(), kind=jnp.bfloat16):
    values = jax.random.normal(rng, shape, jnp.float32) * scale
    if len(shards) > 0:
        values = block_levels(rng, shape, shards, -0.22, 0.18) * values
    return jnp.clip(values, min=-bound, max=bound).astype(kind)


def setup_inputs(seed: int = 0) -> dict:
    streams_of = jax.random.split(jax.random.key(seed), 8)
    return {
        "sep_in": scatter_about(streams_of[0], (N_SUB, LEV, HC, NZ), 1.0, 6.0, ((0, 64), (3, 8)), jnp.float32),
        "inv_blocks": scatter_about(streams_of[1], (N_SUB, BS, BS, NBT), BS ** -0.5, 0.75, ((0, 64), (3, 8))),
        "couple_blocks": scatter_about(streams_of[2], (N_SUB, KI, BS, BS, NBT), (KI * BS) ** -0.5, 0.5, ((0, 64), (4, 8))),
        "face_index": plant(jax.random.randint(streams_of[3], (N_SUB, KI, NBT), 0, FBD), jax.random.fold_in(streams_of[3], 1), 0, FBD - 1).astype(jnp.int32),
        "sep_diag": jnp.clip(1.0 + 2.0 * jax.random.uniform(streams_of[4], (N_SUB, ROWS, NZ), jnp.float32) ** block_levels(streams_of[4], (N_SUB, ROWS, NZ), ((0, 64), (1, 8)), -0.2, 0.2), 1.0, 3.0),
        "sep_couple": scatter_about(streams_of[5], (LEV, KS, BS, BS), (KS * BS) ** -0.5, 0.5, (), jnp.float32),
        "sep_index": plant(jax.random.randint(streams_of[6], (N_SUB, ROWS, NZB, KS), 0, NZB), jax.random.fold_in(streams_of[6], 1), 0, NZB - 1).astype(jnp.int32),
    }


def condense_one(args):
    face_blocks, index_one, couple_one, inverse_one = args
    index_slab = index_one.reshape(KI, N_SEP, NB).transpose(1, 0, 2).reshape(N_SEP, KI * NB)
    picked = jnp.take_along_axis(face_blocks, index_slab[:, :, None], axis=1)
    picked = lax.optimization_barrier(picked.astype(jnp.bfloat16)).astype(jnp.float32)
    picked = picked.reshape(N_SEP, KI, NB, BS)
    coupling = couple_one.astype(jnp.float32).reshape(KI, BS, BS, N_SEP, NB)
    inverse = inverse_one.astype(jnp.float32).reshape(BS, BS, N_SEP, NB)
    driven = jnp.einsum('kijpb,pkbj->pib', coupling, picked, precision=lax.Precision.HIGHEST)
    driven = lax.optimization_barrier(driven.astype(jnp.bfloat16)).astype(jnp.float32)
    solved = jnp.einsum('ijpb,pjb->pib', inverse, driven, precision=lax.Precision.HIGHEST)
    solved = lax.optimization_barrier(solved.astype(jnp.bfloat16)).astype(jnp.float32)
    spread = jnp.einsum('kijpb,pib->pkbj', coupling, solved, precision=lax.Precision.HIGHEST)
    spread = spread.reshape(N_SEP, KI * NB, BS)

    def summed(values, segment_ids):
        return jax.ops.segment_sum(values, segment_ids, num_segments=FBD)

    return jax.vmap(summed)(spread, index_slab)


def reference(sep_in, inv_blocks, couple_blocks, face_index, sep_diag, sep_couple, sep_index):
    subdomains = jnp.arange(N_SUB, dtype=jnp.int32)
    faces = []
    for bisect in range(LEV):
        lower = jnp.bitwise_and(subdomains, jnp.int32(~(1 << bisect)))
        upper = jnp.bitwise_or(subdomains, jnp.int32(1 << bisect))
        faces.append(jnp.concatenate([sep_in[lower, bisect], sep_in[upper, bisect]], axis=1))
    whole = jnp.stack(faces, axis=1)
    face_blocks = whole.reshape(N_SUB, LEV, 2 * HC, N_SEP, ZB, BS).transpose(0, 3, 1, 2, 4, 5)
    face_blocks = face_blocks.reshape(N_SUB, N_SEP, FBD, BS)
    contrib = lax.map(condense_one, (face_blocks, face_index, couple_blocks, inv_blocks))
    contrib = contrib.reshape(N_SUB, N_SEP, LEV, 2 * HC, ZB, BS).transpose(0, 2, 3, 1, 4, 5)
    contrib = contrib.reshape(N_SUB, LEV, 2 * HC, NZ)
    conds = []
    for bisect in range(LEV):
        partner = jnp.bitwise_xor(subdomains, jnp.int32(1 << bisect))
        side = jnp.bitwise_and(jnp.right_shift(subdomains, bisect), 1)
        low_half = contrib[:, bisect, :HC]
        high_half = contrib[:, bisect, HC:]
        own_low = low_half + low_half[partner]
        own_high = high_half + high_half[partner]
        conds.append(jnp.where((side == 0)[:, None, None], own_low, own_high))
    cond = jnp.stack(conds, axis=1).reshape(N_SUB, ROWS, NZ)
    sep_rows = sep_in.reshape(N_SUB, ROWS, NZ)
    row_blocks = sep_rows.reshape(N_SUB, ROWS, NZB, BS)
    chosen = jnp.take_along_axis(row_blocks, sep_index.reshape(N_SUB, ROWS, NZB * KS)[:, :, :, None], axis=2)
    chosen = chosen.reshape(N_SUB, ROWS, NZB, KS, BS)
    level_rows = jnp.arange(ROWS, dtype=jnp.int32) // HC
    couple_rows = sep_couple[level_rows]
    coupled = jnp.einsum('srnkj,rkij->srni', chosen, couple_rows, precision=lax.Precision.HIGHEST)
    return sep_diag * sep_rows + coupled.reshape(N_SUB, ROWS, NZ) - cond
```

```python
import jax
import jax.numpy as jnp
from jax import lax
from jax.experimental import pallas as pl
from jax.experimental.pallas import tpu as pltpu
from jax.sharding import PartitionSpec as P

BS = 64
LEV = 4
NB = 128
NZP = 8
F32 = jnp.float32
BF16 = jnp.bfloat16
MESH = pl.DeviceIdType.MESH
TN = (((0,), (0,)), ((), ()))
NT = (((1,), (1,)), ((), ()))


def one_hot(rows, base, picks):
    place = lax.broadcasted_iota(jnp.int32, (rows, picks.shape[1]), 0) + base
    return jnp.where(place == picks, 1.0, 0.0).astype(BF16)


def halves_by_parity(values, odd):
    return jnp.concatenate([jnp.where(odd, 0.0, values), jnp.where(odd, values, 0.0)], axis=0)


def split(values):
    high = values.astype(BF16)
    return high, (values - high.astype(F32)).astype(BF16)


def kernel(
    sep_hbm, inv_hbm, couple_hbm, fidx_hbm, diag_hbm, w_hbm, sidx_hbm, out_hbm,
    sep_v, inv_v, couple_v, fidx_v, diag_v, w_v, sidx_v, out_v,
    rows_v, face_v, zrows_v, fidx_r, spread_s, spread_r, cond_v, cond_s, cond_r,
    driven_v, solved_v, sidx_t,
    in_sem, out_sem, a_send, a_recv, i_send, i_recv, z_send, z_recv, c_send, c_recv, e_send, e_recv,
):
    s = lax.axis_index("sub")
    z = lax.axis_index("sep")
    side = [lax.rem(lax.div(s, 1 << l), 2) for l in range(LEV)]
    partner = [s + (1 - 2 * side[l]) * (1 << l) for l in range(LEV)]
    own_base = [pl.multiple_of(l * 512 + side[l] * 256, 256) for l in range(LEV)]
    far_base = [pl.multiple_of(l * 512 + (1 - side[l]) * 256, 256) for l in range(LEV)]
    peers = [lax.rem(z + d, NZP) for d in (4, 3, 5, 2, 6, 1, 7)]

    def local(i, src, dst):
        return pltpu.make_async_copy(src, dst, in_sem.at[i])

    loads = [
        local(0, sep_hbm, sep_v),
        local(1, fidx_hbm, fidx_v),
        local(2, couple_hbm, couple_v),
        local(3, inv_hbm, inv_v),
        local(4, sidx_hbm, sidx_v),
        local(5, w_hbm.at[lax.div(z, 2)], w_v),
        local(6, diag_hbm, diag_v),
    ]
    for load in loads:
        load.start()

    barrier = pltpu.get_barrier_semaphore()
    for l in range(LEV):
        pl.semaphore_signal(barrier, inc=1, device_id={"sub": partner[l]}, device_id_type=MESH)
    for peer in peers:
        pl.semaphore_signal(barrier, inc=1, device_id={"sep": peer}, device_id_type=MESH)

    loads[0].wait()
    for l in range(LEV):
        for c in range(8):
            row = sep_v[pl.ds(l * 256 + c, 32, stride=8), :]
            rows_v[pl.ds((l * 8 + c) * 32, 32), :] = row
            face_v[pl.ds(own_base[l] + c * 32, 32), :] = row.astype(BF16)
    loads[1].wait()

    pl.semaphore_wait(barrier, LEV + NZP - 1)

    def to_partner(l, src, dst, send, recv):
        return pltpu.make_async_remote_copy(
            src_ref=src, dst_ref=dst, send_sem=send.at[l], recv_sem=recv.at[l],
            device_id={"sub": partner[l]}, device_id_type=MESH,
        )

    def face_copy(l, base):
        part = face_v.at[pl.ds(base, 256)]
        return to_partner(l, part, part, a_send, a_recv)

    def idx_copy(l):
        return to_partner(l, fidx_v, fidx_r.at[l], i_send, i_recv)

    def spread_copy(l):
        return to_partner(l, spread_s, spread_r.at[l], c_send, c_recv)

    def z_copy(src, dst, slot, place, peer, send, recv, out_slot):
        return pltpu.make_async_remote_copy(
            src_ref=src.at[pl.ds(pl.multiple_of(out_slot * 128, 128), 128)],
            dst_ref=dst.at[pl.ds(pl.multiple_of(place * 128, 128), 128)],
            send_sem=send.at[slot], recv_sem=recv.at[place],
            device_id={"sep": peer}, device_id_type=MESH,
        )

    for l in (3, 2, 1, 0):
        face_copy(l, own_base[l]).start()
    for peer in peers:
        z_copy(rows_v, zrows_v, peer, z, peer, z_send, z_recv, peer).start()
    for l in range(LEV):
        idx_copy(l).start()
    mine = pl.ds(pl.multiple_of(z * 128, 128), 128)
    zrows_v[mine, :] = rows_v[mine, :]

    loads[4].wait()
    block = jnp.concatenate([sidx_v[r] for r in range(4)] * 16, axis=0)
    sidx_t[...] = jnp.transpose(lax.rem(block, 2) * 256 + lax.div(block, 2))

    index = jnp.concatenate([fidx_v[0:1, :], fidx_v[1:2, :]], axis=1)
    odd = lax.rem(index, 2) == 1
    place = lax.div(index, 2)

    def picked_from(base):
        part = face_v[pl.ds(base, 256), :]
        return lax.dot_general(part, one_hot(256, base, place), TN, preferred_element_type=F32)

    picked = picked_from(own_base[0])
    for l in range(1, LEV):
        picked += picked_from(own_base[l])
    loads[2].wait()
    loads[3].wait()
    for l in range(LEV):
        face_copy(l, far_base[l]).wait_recv()
        picked += picked_from(far_base[l])
    picked = jnp.where(odd, picked[BS:], picked[:BS])
    first, second = picked[:, :NB], picked[:, NB:]

    def rows_of(i, body):
        return jnp.concatenate([body(i * 8 + e) for e in range(8)], axis=0)

    def drive(i, carry):
        def one(row):
            total = couple_v[0, row].astype(F32) * first + couple_v[1, row].astype(F32) * second
            return jnp.sum(total, axis=0, keepdims=True)
        driven_v[pl.ds(pl.multiple_of(i * 8, 8), 8), :] = rows_of(i, one)
        return carry

    lax.fori_loop(0, 8, drive, 0)
    driven = driven_v[...].astype(BF16).astype(F32)

    def solve(i, carry):
        def one(row):
            return jnp.sum(inv_v[row].astype(F32) * driven, axis=0, keepdims=True)
        solved_v[pl.ds(pl.multiple_of(i * 8, 8), 8), :] = rows_of(i, one).astype(BF16).astype(F32)
        return carry

    lax.fori_loop(0, 8, solve, 0)

    def spread_step(i, carry):
        low, high = carry
        part = solved_v[pl.ds(pl.multiple_of(i * 8, 8), 8), :]
        for e in range(8):
            row = part[e : e + 1, :]
            low += couple_v[0, i * 8 + e].astype(F32) * row
            high += couple_v[1, i * 8 + e].astype(F32) * row
        return low, high

    zero = jnp.zeros((BS, NB), F32)
    low, high = lax.fori_loop(0, 8, spread_step, (zero, zero))
    spread_s[pl.ds(0, BS), :] = low.astype(BF16)
    spread_s[pl.ds(BS, BS), :] = high.astype(BF16)
    for l in (3, 2, 1, 0):
        spread_copy(l).start()

    own_high, own_low = split(halves_by_parity(jnp.concatenate([low, high], axis=1), odd))
    for l in range(LEV):
        table = one_hot(256, own_base[l], place)
        part = lax.dot_general(table, own_high, NT, preferred_element_type=F32)
        part += lax.dot_general(table, own_low, NT, preferred_element_type=F32)
        cond_v[pl.ds(l * 256, 256), :] = part

    def cond_copy(peer, place):
        return z_copy(cond_s, cond_r, peer, place, peer, e_send, e_recv, peer)

    for l in range(LEV):
        idx_copy(l).wait_recv()
        got = jnp.concatenate([fidx_r[l, 0:1, :], fidx_r[l, 1:2, :]], axis=1)
        spread_copy(l).wait_recv()
        values = spread_r[l].astype(F32)
        values = jnp.concatenate([values[:BS], values[BS:]], axis=1)
        values = halves_by_parity(values, lax.rem(got, 2) == 1).astype(BF16)
        table = one_hot(256, own_base[l], lax.div(got, 2))
        part = cond_v[pl.ds(l * 256, 256), :] + lax.dot_general(
            table, values, NT, preferred_element_type=F32
        )
        cond_s[pl.ds(l * 256, 256), :] = part.astype(BF16)
        for h in range(2):
            q = 2 * l + h

            @pl.when(z != q)
            def _():
                z_copy(cond_s, cond_r, q, z, q, e_send, e_recv, q).start()

            @pl.when(z == q)
            def _():
                cond_r[pl.ds(q * 128, 128), :] = cond_s[pl.ds(q * 128, 128), :]

    loads[5].wait()
    loads[6].wait()
    empty = jnp.zeros((BS, BS), F32)
    weights = []
    for j in range(2):
        w = w_v[j]
        left = jnp.concatenate([w, empty], axis=1)
        right = jnp.concatenate([empty, w], axis=1)
        weights += [left, left, right, right]
    w_high, w_low = split(jnp.concatenate(weights, axis=0))
    first_half = lax.broadcasted_iota(jnp.int32, (256, 128), 1) < BS
    column = lax.broadcasted_iota(jnp.int32, (512, 512), 1)
    picks = jnp.concatenate([sidx_t[pl.ds(e, 256, stride=2), :] for e in range(2)], axis=0)

    for peer in peers:
        z_copy(rows_v, zrows_v, peer, peer, peer, z_send, z_recv, peer).wait_recv()
    for r in range(4):
        x = jnp.concatenate([zrows_v[pl.ds(p * 128 + r * 32, 32), :] for p in range(NZP)], axis=0)
        x_high, x_low = split(x)
        y = lax.dot_general(x_high, w_high, NT, preferred_element_type=F32)
        y += lax.dot_general(x_low, w_high, NT, preferred_element_type=F32)
        y += lax.dot_general(x_high, w_low, NT, preferred_element_type=F32)
        total = None
        for j in range(2):
            table = jnp.where(column == picks[:, 2 * r + j : 2 * r + j + 1], 1.0, 0.0).astype(BF16)
            parts = []
            for half in range(2):
                g = 2 * j + half
                y_high, y_low = split(y[:, g * 128 : (g + 1) * 128])
                parts.append(jnp.where(first_half, y_high.astype(F32), y_low.astype(F32)).astype(BF16))
            term = jnp.dot(table, jnp.concatenate(parts, axis=0), preferred_element_type=F32)
            total = term if total is None else total + term
        total = total + pltpu.roll(total, BS, 1)
        coupled = jnp.where(first_half, total[:256], total[256:])
        spot = pl.ds(r, 256, stride=4)
        out_v[spot, :] = diag_v[spot, :] * x + coupled

    def finish(p):
        for r in range(4):
            spot = pl.ds(p * 128 + r, 32, stride=4)
            part = cond_r[pl.ds(pl.multiple_of(p * 128 + r * 32, 32), 32), :]
            out_v[spot, :] = out_v[spot, :] - part.astype(F32)
        chunk = pl.ds(pl.multiple_of(p * 128, 128), 128)
        pltpu.make_async_copy(out_v.at[chunk], out_hbm.at[chunk], out_sem.at[p]).start()

    finish(z)
    for peer in (peers[6], peers[5], peers[4], peers[3], peers[2], peers[1], peers[0]):
        cond_copy(peer, peer).wait_recv()
        finish(peer)

    for l in range(LEV):
        face_copy(l, own_base[l]).wait_send()
        idx_copy(l).wait_send()
        spread_copy(l).wait_send()
    for peer in peers:
        z_copy(rows_v, zrows_v, peer, z, peer, z_send, z_recv, peer).wait_send()
        cond_copy(peer, z).wait_send()
    for p in range(NZP):
        chunk = pl.ds(p * 128, 128)
        pltpu.make_async_copy(out_v.at[chunk], out_hbm.at[chunk], out_sem.at[p]).wait()


def local(sep_in, inv_blocks, couple_blocks, face_index, sep_diag, sep_couple, sep_index):
    sep_tiles = sep_in.reshape(4, 8, 32, 128).transpose(0, 2, 1, 3).reshape(1024, 128)
    diag_tiles = sep_diag.reshape(4, 256, 128).transpose(1, 0, 2).reshape(1024, 128)
    picks = sep_index.reshape(4, 512, 2).transpose(0, 2, 1)
    dma = pltpu.SemaphoreType.DMA
    out = pl.pallas_call(
        kernel,
        out_shape=jax.ShapeDtypeStruct((1024, 128), F32),
        in_specs=[pl.BlockSpec(memory_space=pl.ANY)] * 7,
        out_specs=pl.BlockSpec(memory_space=pl.ANY),
        scratch_shapes=[
            pltpu.VMEM((1024, 128), F32),
            pltpu.VMEM((64, 64, 128), BF16),
            pltpu.VMEM((2, 64, 64, 128), BF16),
            pltpu.VMEM((2, 128), jnp.int32),
            pltpu.VMEM((1024, 128), F32),
            pltpu.VMEM((2, 64, 64), F32),
            pltpu.VMEM((4, 2, 512), jnp.int32),
            pltpu.VMEM((1024, 128), F32),
            pltpu.VMEM((1024, 128), F32),
            pltpu.VMEM((2048, 128), BF16),
            pltpu.VMEM((1024, 128), F32),
            pltpu.VMEM((4, 2, 128), jnp.int32),
            pltpu.VMEM((128, 128), BF16),
            pltpu.VMEM((4, 128, 128), BF16),
            pltpu.VMEM((1024, 128), F32),
            pltpu.VMEM((1024, 128), BF16),
            pltpu.VMEM((1024, 128), BF16),
            pltpu.VMEM((64, 128), F32),
            pltpu.VMEM((64, 128), F32),
            pltpu.VMEM((512, 128), jnp.int32),
            dma((7,)),
            dma((8,)),
            dma((4,)),
            dma((4,)),
            dma((4,)),
            dma((4,)),
            dma((8,)),
            dma((8,)),
            dma((4,)),
            dma((4,)),
            dma((8,)),
            dma((8,)),
        ],
        compiler_params=pltpu.CompilerParams(
            collective_id=0, has_side_effects=True, vmem_limit_bytes=62 * 1024 * 1024
        ),
        cost_estimate=pl.CostEstimate(flops=3_000_000_000, bytes_accessed=5_000_000, transcendentals=0),
    )(
        sep_tiles, inv_blocks.reshape(64, 64, 128), couple_blocks.reshape(2, 64, 64, 128),
        face_index.reshape(2, 128), diag_tiles, sep_couple, picks,
    )
    return out.reshape(256, 4, 128).transpose(1, 0, 2).reshape(1, 4, 32768)


def solution(mesh):
    return jax.shard_map(
        local,
        mesh=mesh,
        in_specs=(
            P("sub", None, None, "sep"),
            P("sub", None, None, "sep"),
            P("sub", None, None, None, "sep"),
            P("sub", None, "sep"),
            P("sub", "sep", None),
            P(),
            P("sub", "sep", None, None),
        ),
        out_specs=P("sub", "sep", None),
        check_vma=False,
    )
```

```python
import jax
import jax.numpy as jnp
from jax import lax
from jax.experimental import pallas as pl
from jax.experimental.pallas import tpu as pltpu
from jax.sharding import PartitionSpec as P

BS = 64
LEV = 4
NB = 128
NZP = 8
F32 = jnp.float32
BF16 = jnp.bfloat16
MESH = pl.DeviceIdType.MESH
TN = (((0,), (0,)), ((), ()))
NT = (((1,), (1,)), ((), ()))


def one_hot(rows, base, picks):
    place = lax.broadcasted_iota(jnp.int32, (rows, picks.shape[1]), 0) + base
    return jnp.where(place == picks, 1.0, 0.0).astype(BF16)


def halves_by_parity(values, odd):
    return jnp.concatenate([jnp.where(odd, 0.0, values), jnp.where(odd, values, 0.0)], axis=0)


def split(values):
    high = values.astype(BF16)
    return high, (values - high.astype(F32)).astype(BF16)


def kernel(
    sep_hbm, inv_hbm, couple_hbm, fidx_hbm, diag_hbm, w_hbm, sidx_hbm, out_v, cond_r,
    sep_v, inv_v, couple_v, fidx_v, diag_v, w_v, sidx_v,
    rows_v, face_v, far_v, zrows_v, fidx_r, pick_s, pick_r, spread_s, spread_r, cond_v, cond_s,
    driven_v, solved_v, sidx_t,
    in_sem, a_send, a_recv, i_send, i_recv, z_send, z_recv, c_send, c_recv, e_send, e_recv,
):
    s = lax.axis_index("sub")
    z = lax.axis_index("sep")
    side = [lax.rem(lax.div(s, 1 << l), 2) for l in range(LEV)]
    partner = [s + (1 - 2 * side[l]) * (1 << l) for l in range(LEV)]
    own_base = [pl.multiple_of(l * 512 + side[l] * 256, 256) for l in range(LEV)]
    far_base = (LEV - 1) * 512 + (1 - side[LEV - 1]) * 256
    peers = [lax.rem(z + d, NZP) for d in (4, 3, 5, 2, 6, 1, 7)]

    def local(i, src, dst):
        return pltpu.make_async_copy(src, dst, in_sem.at[i])

    loads = [
        local(0, sep_hbm, sep_v),
        local(1, fidx_hbm, fidx_v),
        local(2, couple_hbm, couple_v),
        local(3, inv_hbm, inv_v),
        local(4, sidx_hbm, sidx_v),
        local(5, w_hbm.at[lax.div(z, 2)], w_v),
        local(6, diag_hbm, diag_v),
    ]
    for load in loads:
        load.start()

    barrier = pltpu.get_barrier_semaphore()
    for l in range(LEV):
        pl.semaphore_signal(barrier, inc=1, device_id={"sub": partner[l]}, device_id_type=MESH)
    for peer in peers:
        pl.semaphore_signal(barrier, inc=1, device_id={"sep": peer}, device_id_type=MESH)

    loads[0].wait()
    for l in range(LEV):
        for c in range(8):
            row = sep_v[pl.ds(l * 256 + c, 32, stride=8), :]
            rows_v[pl.ds((l * 8 + c) * 32, 32), :] = row
            face_v[pl.ds((l * 8 + c) * 32, 32), :] = row.astype(BF16)
    loads[1].wait()

    pl.semaphore_wait(barrier, LEV + NZP - 1)

    def to_partner(l, src, dst, send, recv):
        return pltpu.make_async_remote_copy(
            src_ref=src, dst_ref=dst, send_sem=send.at[l], recv_sem=recv.at[l],
            device_id={"sub": partner[l]}, device_id_type=MESH,
        )

    def face_copy():
        return to_partner(LEV - 1, face_v.at[pl.ds((LEV - 1) * 256, 256)], far_v, a_send, a_recv)

    def pick_copy(l):
        return to_partner(l, pick_s.at[l], pick_r.at[l], a_send, a_recv)

    def idx_copy(l):
        return to_partner(l, fidx_v, fidx_r.at[l], i_send, i_recv)

    def spread_copy(l):
        return to_partner(l, spread_s, spread_r.at[l], c_send, c_recv)

    def z_copy(src, dst, slot, place, peer, send, recv, out_slot):
        return pltpu.make_async_remote_copy(
            src_ref=src.at[pl.ds(pl.multiple_of(out_slot * 128, 128), 128)],
            dst_ref=dst.at[pl.ds(pl.multiple_of(place * 128, 128), 128)],
            send_sem=send.at[slot], recv_sem=recv.at[place],
            device_id={"sep": peer}, device_id_type=MESH,
        )

    face_copy().start()
    for l in (2, 1, 0, 3):
        idx_copy(l).start()
    for peer in peers:
        z_copy(rows_v, zrows_v, peer, z, peer, z_send, z_recv, peer).start()
    mine = pl.ds(pl.multiple_of(z * 128, 128), 128)
    zrows_v[mine, :] = rows_v[mine, :]

    loads[4].wait()
    block = jnp.concatenate([sidx_v[r] for r in range(4)] * 16, axis=0)
    sidx_t[...] = jnp.transpose(lax.rem(block, 2) * 256 + lax.div(block, 2))

    def places(pair):
        both = jnp.concatenate([pair[0:1, :], pair[1:2, :]], axis=1)
        return lax.rem(both, 2) == 1, lax.div(both, 2)

    def picked_from(part, base, at):
        return lax.dot_general(part, one_hot(256, base, at), TN, preferred_element_type=F32)

    odd, place = places(fidx_v[...])
    for l in (0, 1, 2):
        idx_copy(l).wait_recv()
        got_odd, got_place = places(fidx_r[l])
        got = picked_from(face_v[pl.ds(l * 256, 256), :], own_base[l], got_place)
        got = jnp.where(got_odd, got[BS:], got[:BS])
        pick_s[l] = jnp.concatenate([got[:, :NB], got[:, NB:]], axis=0).astype(BF16)
        pick_copy(l).start()
    picked = picked_from(face_v[pl.ds(0, 256), :], own_base[0], place)
    for l in range(1, LEV):
        picked += picked_from(face_v[pl.ds(l * 256, 256), :], own_base[l], place)
    loads[2].wait()
    loads[3].wait()
    near = jnp.zeros((2 * BS, NB), F32)
    for l in (0, 1, 2):
        pick_copy(l).wait_recv()
        near += pick_r[l].astype(F32)
    face_copy().wait_recv()
    picked += picked_from(far_v[...], far_base, place)
    picked = jnp.where(odd, picked[BS:], picked[:BS])
    picked += jnp.concatenate([near[:BS], near[BS:]], axis=1)
    first, second = picked[:, :NB], picked[:, NB:]

    def rows_of(i, body):
        return jnp.concatenate([body(i * 8 + e) for e in range(8)], axis=0)

    def drive(i, carry):
        def one(row):
            total = couple_v[0, row].astype(F32) * first + couple_v[1, row].astype(F32) * second
            return jnp.sum(total, axis=0, keepdims=True)
        driven_v[pl.ds(pl.multiple_of(i * 8, 8), 8), :] = rows_of(i, one)
        return carry

    lax.fori_loop(0, 8, drive, 0)
    driven = driven_v[...].astype(BF16).astype(F32)

    def solve(i, carry):
        def one(row):
            return jnp.sum(inv_v[row].astype(F32) * driven, axis=0, keepdims=True)
        solved_v[pl.ds(pl.multiple_of(i * 8, 8), 8), :] = rows_of(i, one).astype(BF16).astype(F32)
        return carry

    lax.fori_loop(0, 8, solve, 0)

    def spread_step(i, carry):
        low, high = carry
        part = solved_v[pl.ds(pl.multiple_of(i * 8, 8), 8), :]
        for e in range(8):
            row = part[e : e + 1, :]
            low += couple_v[0, i * 8 + e].astype(F32) * row
            high += couple_v[1, i * 8 + e].astype(F32) * row
        return low, high

    zero = jnp.zeros((BS, NB), F32)
    low, high = lax.fori_loop(0, 8, spread_step, (zero, zero))
    spread_s[pl.ds(0, BS), :] = low.astype(BF16)
    spread_s[pl.ds(BS, BS), :] = high.astype(BF16)
    for l in (3, 2, 1, 0):
        spread_copy(l).start()

    own_high, own_low = split(halves_by_parity(jnp.concatenate([low, high], axis=1), odd))
    for l in range(LEV):
        table = one_hot(256, own_base[l], place)
        part = lax.dot_general(table, own_high, NT, preferred_element_type=F32)
        part += lax.dot_general(table, own_low, NT, preferred_element_type=F32)
        cond_v[pl.ds(l * 256, 256), :] = part

    def cond_copy(peer, place):
        return z_copy(cond_s, cond_r, peer, place, peer, e_send, e_recv, peer)

    for l in range(LEV):
        if l == LEV - 1:
            idx_copy(l).wait_recv()
        got_odd, got_place = places(fidx_r[l])
        spread_copy(l).wait_recv()
        values = spread_r[l].astype(F32)
        values = jnp.concatenate([values[:BS], values[BS:]], axis=1)
        values = halves_by_parity(values, got_odd).astype(BF16)
        table = one_hot(256, own_base[l], got_place)
        part = cond_v[pl.ds(l * 256, 256), :] + lax.dot_general(
            table, values, NT, preferred_element_type=F32
        )
        cond_s[pl.ds(l * 256, 256), :] = part.astype(BF16)
        for h in range(2):
            q = 2 * l + h

            @pl.when(z != q)
            def _():
                z_copy(cond_s, cond_r, q, z, q, e_send, e_recv, q).start()

            @pl.when(z == q)
            def _():
                cond_r[pl.ds(q * 128, 128), :] = cond_s[pl.ds(q * 128, 128), :]

    loads[5].wait()
    loads[6].wait()
    empty = jnp.zeros((BS, BS), F32)
    weights = []
    for j in range(2):
        w = w_v[j]
        left = jnp.concatenate([w, empty], axis=1)
        right = jnp.concatenate([empty, w], axis=1)
        weights += [left, left, right, right]
    w_high, w_low = split(jnp.concatenate(weights, axis=0))
    first_half = lax.broadcasted_iota(jnp.int32, (256, 128), 1) < BS
    column = lax.broadcasted_iota(jnp.int32, (512, 512), 1)
    picks = jnp.concatenate([sidx_t[pl.ds(e, 256, stride=2), :] for e in range(2)], axis=0)

    for peer in peers:
        z_copy(rows_v, zrows_v, peer, peer, peer, z_send, z_recv, peer).wait_recv()
    for r in range(4):
        x = jnp.concatenate([zrows_v[pl.ds(p * 128 + r * 32, 32), :] for p in range(NZP)], axis=0)
        x_high, x_low = split(x)
        y = lax.dot_general(x_high, w_high, NT, preferred_element_type=F32)
        y += lax.dot_general(x_low, w_high, NT, preferred_element_type=F32)
        y += lax.dot_general(x_high, w_low, NT, preferred_element_type=F32)
        total = None
        for j in range(2):
            table = jnp.where(column == picks[:, 2 * r + j : 2 * r + j + 1], 1.0, 0.0).astype(BF16)
            parts = []
            for half in range(2):
                g = 2 * j + half
                y_high, y_low = split(y[:, g * 128 : (g + 1) * 128])
                parts.append(jnp.where(first_half, y_high.astype(F32), y_low.astype(F32)).astype(BF16))
            term = jnp.dot(table, jnp.concatenate(parts, axis=0), preferred_element_type=F32)
            total = term if total is None else total + term
        total = total + pltpu.roll(total, BS, 1)
        coupled = jnp.where(first_half, total[:256], total[256:])
        spot = pl.ds(r, 256, stride=4)
        out_v[spot, :] = diag_v[spot, :] * x + coupled

    for peer in peers:
        cond_copy(peer, peer).wait_recv()
    for l in range(LEV):
        (face_copy() if l == LEV - 1 else pick_copy(l)).wait_send()
        idx_copy(l).wait_send()
        spread_copy(l).wait_send()
    for peer in peers:
        z_copy(rows_v, zrows_v, peer, z, peer, z_send, z_recv, peer).wait_send()
        cond_copy(peer, z).wait_send()


def last(part, cond, out_hbm, out_v, sem):
    copies = []
    for p in range(NZP):
        chunk = pl.ds(p * 128, 128)
        for r in range(4):
            spot = pl.ds(p * 128 + r, 32, stride=4)
            out_v[spot, :] = part[spot, :] - cond[pl.ds(p * 128 + r * 32, 32), :].astype(F32)
        copies.append(pltpu.make_async_copy(out_v.at[chunk], out_hbm.at[chunk], sem.at[p]))
        copies[-1].start()
    for copy in copies:
        copy.wait()


def local(sep_in, inv_blocks, couple_blocks, face_index, sep_diag, sep_couple, sep_index):
    sep_tiles = sep_in.reshape(4, 8, 32, 128).transpose(0, 2, 1, 3).reshape(1024, 128)
    diag_tiles = sep_diag.reshape(4, 256, 128).transpose(1, 0, 2).reshape(1024, 128)
    picks = sep_index.reshape(4, 512, 2).transpose(0, 2, 1)
    dma = pltpu.SemaphoreType.DMA
    part, cond = pl.pallas_call(
        kernel,
        out_shape=(pltpu.VMEM((1024, 128), F32), pltpu.VMEM((1024, 128), BF16)),
        in_specs=[pl.BlockSpec(memory_space=pl.ANY)] * 7,
        out_specs=(pl.BlockSpec(memory_space=pltpu.VMEM), pl.BlockSpec(memory_space=pltpu.VMEM)),
        scratch_shapes=[
            pltpu.VMEM((1024, 128), F32),
            pltpu.VMEM((64, 64, 128), BF16),
            pltpu.VMEM((2, 64, 64, 128), BF16),
            pltpu.VMEM((2, 128), jnp.int32),
            pltpu.VMEM((1024, 128), F32),
            pltpu.VMEM((2, 64, 64), F32),
            pltpu.VMEM((4, 2, 512), jnp.int32),
            pltpu.VMEM((1024, 128), F32),
            pltpu.VMEM((1024, 128), BF16),
            pltpu.VMEM((256, 128), BF16),
            pltpu.VMEM((1024, 128), F32),
            pltpu.VMEM((4, 2, 128), jnp.int32),
            pltpu.VMEM((3, 128, 128), BF16),
            pltpu.VMEM((3, 128, 128), BF16),
            pltpu.VMEM((128, 128), BF16),
            pltpu.VMEM((4, 128, 128), BF16),
            pltpu.VMEM((1024, 128), F32),
            pltpu.VMEM((1024, 128), BF16),
            pltpu.VMEM((64, 128), F32),
            pltpu.VMEM((64, 128), F32),
            pltpu.VMEM((512, 128), jnp.int32),
            dma((7,)),
            dma((4,)),
            dma((4,)),
            dma((4,)),
            dma((4,)),
            dma((8,)),
            dma((8,)),
            dma((4,)),
            dma((4,)),
            dma((8,)),
            dma((8,)),
        ],
        compiler_params=pltpu.CompilerParams(
            collective_id=0, has_side_effects=True, vmem_limit_bytes=62 * 1024 * 1024
        ),
        cost_estimate=pl.CostEstimate(flops=3_000_000_000, bytes_accessed=5_000_000, transcendentals=0),
    )(
        sep_tiles, inv_blocks.reshape(64, 64, 128), couple_blocks.reshape(2, 64, 64, 128),
        face_index.reshape(2, 128), diag_tiles, sep_couple, picks,
    )
    out = pl.pallas_call(
        last,
        out_shape=jax.ShapeDtypeStruct((1024, 128), F32),
        in_specs=[pl.BlockSpec(memory_space=pltpu.VMEM)] * 2,
        out_specs=pl.BlockSpec(memory_space=pl.ANY),
        scratch_shapes=[pltpu.VMEM((1024, 128), F32), dma((8,))],
    )(
        pltpu.with_memory_space_constraint(part, pltpu.VMEM),
        pltpu.with_memory_space_constraint(cond, pltpu.VMEM),
    )
    return out.reshape(256, 4, 128).transpose(1, 0, 2).reshape(1, 4, 32768)


def solution(mesh):
    return jax.shard_map(
        local,
        mesh=mesh,
        in_specs=(
            P("sub", None, None, "sep"),
            P("sub", None, None, "sep"),
            P("sub", None, None, None, "sep"),
            P("sub", None, "sep"),
            P("sub", "sep", None),
            P(),
            P("sub", "sep", None, None),
        ),
        out_specs=P("sub", "sep", None),
        check_vma=False,
    )
```

```python
import jax
import jax.numpy as jnp
from jax import lax
from jax.experimental import pallas as pl
from jax.experimental.pallas import tpu as pltpu
from jax.sharding import PartitionSpec as P

BS = 64
LEV = 4
NB = 128
NZP = 8
F32 = jnp.float32
BF16 = jnp.bfloat16
MESH = pl.DeviceIdType.MESH
TN = (((0,), (0,)), ((), ()))
NT = (((1,), (1,)), ((), ()))


def one_hot(rows, base, picks):
    place = lax.broadcasted_iota(jnp.int32, (rows, picks.shape[1]), 0) + base
    return jnp.where(place == picks, 1.0, 0.0).astype(BF16)


def halves_by_parity(values, odd):
    return jnp.concatenate([jnp.where(odd, 0.0, values), jnp.where(odd, values, 0.0)], axis=0)


def split(values):
    high = values.astype(BF16)
    return high, (values - high.astype(F32)).astype(BF16)


def kernel(
    sep_hbm, inv_hbm, couple_hbm, fidx_hbm, diag_hbm, w_hbm, sidx_hbm, out_v, cond_r,
    sep_v, inv_v, couple_v, fidx_v, diag_v, w_v, sidx_v,
    rows_v, face_v, far_v, zrows_v, fidx_r, pick_s, pick_r, spread_s, spread_r, cond_v, cond_s,
    driven_v, solved_v, sidx_t,
    in_sem, a_send, a_recv, i_send, i_recv, z_send, z_recv, c_send, c_recv, e_send, e_recv,
):
    s = lax.axis_index("sub")
    z = lax.axis_index("sep")
    side = [lax.rem(lax.div(s, 1 << l), 2) for l in range(LEV)]
    partner = [s + (1 - 2 * side[l]) * (1 << l) for l in range(LEV)]
    own_base = [pl.multiple_of(l * 512 + side[l] * 256, 256) for l in range(LEV)]
    far_base = (LEV - 1) * 512 + (1 - side[LEV - 1]) * 256
    peers = [lax.rem(z + d, NZP) for d in (4, 3, 5, 2, 6, 1, 7)]

    def local(i, src, dst):
        return pltpu.make_async_copy(src, dst, in_sem.at[i])

    loads = [
        local(0, sep_hbm, sep_v),
        local(1, fidx_hbm, fidx_v),
        local(2, couple_hbm, couple_v),
        local(3, inv_hbm, inv_v),
        local(4, sidx_hbm, sidx_v),
        local(5, w_hbm.at[lax.div(z, 2)], w_v),
        local(6, diag_hbm, diag_v),
    ]
    for load in loads:
        load.start()

    barrier = pltpu.get_barrier_semaphore()
    for l in (3, 2, 1, 0):
        pl.semaphore_signal(barrier, inc=1, device_id={"sub": partner[l]}, device_id_type=MESH)
    for peer in peers:
        pl.semaphore_signal(barrier, inc=1, device_id={"sep": peer}, device_id_type=MESH)

    loads[0].wait()
    for l in range(LEV):
        for c in range(8):
            row = sep_v[pl.ds(l * 256 + c, 32, stride=8), :]
            rows_v[pl.ds((l * 8 + c) * 32, 32), :] = row
            face_v[pl.ds((l * 8 + c) * 32, 32), :] = row.astype(BF16)
    loads[1].wait()

    pl.semaphore_wait(barrier, LEV + NZP - 1)

    def to_partner(l, src, dst, send, recv):
        return pltpu.make_async_remote_copy(
            src_ref=src, dst_ref=dst, send_sem=send.at[l], recv_sem=recv.at[l],
            device_id={"sub": partner[l]}, device_id_type=MESH,
        )

    def face_copy():
        return to_partner(LEV - 1, face_v.at[pl.ds((LEV - 1) * 256, 256)], far_v, a_send, a_recv)

    def pick_copy(l):
        return to_partner(l, pick_s.at[l], pick_r.at[l], a_send, a_recv)

    def idx_copy(l):
        return to_partner(l, fidx_v, fidx_r.at[l], i_send, i_recv)

    def spread_copy(l):
        return to_partner(l, spread_s, spread_r.at[l], c_send, c_recv)

    def z_copy(src, dst, slot, place, peer, send, recv, out_slot):
        return pltpu.make_async_remote_copy(
            src_ref=src.at[pl.ds(pl.multiple_of(out_slot * 128, 128), 128)],
            dst_ref=dst.at[pl.ds(pl.multiple_of(place * 128, 128), 128)],
            send_sem=send.at[slot], recv_sem=recv.at[place],
            device_id={"sep": peer}, device_id_type=MESH,
        )

    for l in (2, 1, 0):
        idx_copy(l).start()
    face_copy().start()
    idx_copy(LEV - 1).start()
    for peer in peers:
        z_copy(rows_v, zrows_v, peer, z, peer, z_send, z_recv, peer).start()
    mine = pl.ds(pl.multiple_of(z * 128, 128), 128)
    zrows_v[mine, :] = rows_v[mine, :]

    loads[4].wait()
    block = jnp.concatenate([sidx_v[r] for r in range(4)] * 16, axis=0)
    sidx_t[...] = jnp.transpose(lax.rem(block, 2) * 256 + lax.div(block, 2))

    def places(pair):
        both = jnp.concatenate([pair[0:1, :], pair[1:2, :]], axis=1)
        return lax.rem(both, 2) == 1, lax.div(both, 2)

    def picked_from(part, base, at):
        return lax.dot_general(part, one_hot(256, base, at), TN, preferred_element_type=F32)

    odd, place = places(fidx_v[...])
    for l in (0, 1, 2):
        idx_copy(l).wait_recv()
        got_odd, got_place = places(fidx_r[l])
        got = picked_from(face_v[pl.ds(l * 256, 256), :], own_base[l], got_place)
        got = jnp.where(got_odd, got[BS:], got[:BS])
        pick_s[l] = jnp.concatenate([got[:, :NB], got[:, NB:]], axis=0).astype(BF16)
        pick_copy(l).start()
    picked = picked_from(face_v[pl.ds(0, 256), :], own_base[0], place)
    for l in range(1, LEV):
        picked += picked_from(face_v[pl.ds(l * 256, 256), :], own_base[l], place)
    loads[2].wait()
    loads[3].wait()
    near = jnp.zeros((2 * BS, NB), F32)
    for l in (0, 1, 2):
        pick_copy(l).wait_recv()
        near += pick_r[l].astype(F32)
    face_copy().wait_recv()
    picked += picked_from(far_v[...], far_base, place)
    picked = jnp.where(odd, picked[BS:], picked[:BS])
    picked += jnp.concatenate([near[:BS], near[BS:]], axis=1)
    first, second = picked[:, :NB], picked[:, NB:]

    def rows_of(i, body):
        return jnp.concatenate([body(i * 8 + e) for e in range(8)], axis=0)

    def drive(i, carry):
        def one(row):
            total = couple_v[0, row].astype(F32) * first + couple_v[1, row].astype(F32) * second
            return jnp.sum(total, axis=0, keepdims=True)
        driven_v[pl.ds(pl.multiple_of(i * 8, 8), 8), :] = rows_of(i, one)
        return carry

    lax.fori_loop(0, 8, drive, 0, unroll=2)
    driven = driven_v[...].astype(BF16).astype(F32)

    def solve(i, carry):
        def one(row):
            return jnp.sum(inv_v[row].astype(F32) * driven, axis=0, keepdims=True)
        solved_v[pl.ds(pl.multiple_of(i * 8, 8), 8), :] = rows_of(i, one).astype(BF16).astype(F32)
        return carry

    lax.fori_loop(0, 8, solve, 0, unroll=2)

    def spread_step(i, carry):
        low, high = carry
        part = solved_v[pl.ds(pl.multiple_of(i * 8, 8), 8), :]
        for e in range(8):
            row = part[e : e + 1, :]
            low += couple_v[0, i * 8 + e].astype(F32) * row
            high += couple_v[1, i * 8 + e].astype(F32) * row
        return low, high

    zero = jnp.zeros((BS, NB), F32)
    low, high = lax.fori_loop(0, 8, spread_step, (zero, zero), unroll=2)
    spread_s[pl.ds(0, BS), :] = low.astype(BF16)
    spread_s[pl.ds(BS, BS), :] = high.astype(BF16)
    for l in (3, 2, 1, 0):
        spread_copy(l).start()

    own_high, own_low = split(halves_by_parity(jnp.concatenate([low, high], axis=1), odd))
    for l in range(LEV):
        table = one_hot(256, own_base[l], place)
        part = lax.dot_general(table, own_high, NT, preferred_element_type=F32)
        part += lax.dot_general(table, own_low, NT, preferred_element_type=F32)
        cond_v[pl.ds(l * 256, 256), :] = part

    def cond_copy(peer, place):
        return z_copy(cond_s, cond_r, peer, place, peer, e_send, e_recv, peer)

    for l in range(LEV):
        if l == LEV - 1:
            idx_copy(l).wait_recv()
        got_odd, got_place = places(fidx_r[l])
        spread_copy(l).wait_recv()
        values = spread_r[l].astype(F32)
        values = jnp.concatenate([values[:BS], values[BS:]], axis=1)
        values = halves_by_parity(values, got_odd).astype(BF16)
        table = one_hot(256, own_base[l], got_place)
        part = cond_v[pl.ds(l * 256, 256), :] + lax.dot_general(
            table, values, NT, preferred_element_type=F32
        )
        cond_s[pl.ds(l * 256, 256), :] = part.astype(BF16)
        for h in range(2):
            q = 2 * l + h

            @pl.when(z != q)
            def _():
                z_copy(cond_s, cond_r, q, z, q, e_send, e_recv, q).start()

            @pl.when(z == q)
            def _():
                cond_r[pl.ds(q * 128, 128), :] = cond_s[pl.ds(q * 128, 128), :]

    loads[5].wait()
    loads[6].wait()
    empty = jnp.zeros((BS, BS), F32)
    weights = []
    for j in range(2):
        w = w_v[j]
        left = jnp.concatenate([w, empty], axis=1)
        right = jnp.concatenate([empty, w], axis=1)
        weights += [left, left, right, right]
    w_high, w_low = split(jnp.concatenate(weights, axis=0))
    first_half = lax.broadcasted_iota(jnp.int32, (256, 128), 1) < BS
    column = lax.broadcasted_iota(jnp.int32, (512, 512), 1)
    picks = jnp.concatenate([sidx_t[pl.ds(e, 256, stride=2), :] for e in range(2)], axis=0)

    for peer in peers:
        z_copy(rows_v, zrows_v, peer, peer, peer, z_send, z_recv, peer).wait_recv()
    for r in range(4):
        x = jnp.concatenate([zrows_v[pl.ds(p * 128 + r * 32, 32), :] for p in range(NZP)], axis=0)
        x_high, x_low = split(x)
        y = lax.dot_general(x_high, w_high, NT, preferred_element_type=F32)
        y += lax.dot_general(x_low, w_high, NT, preferred_element_type=F32)
        y += lax.dot_general(x_high, w_low, NT, preferred_element_type=F32)
        total = None
        for j in range(2):
            table = jnp.where(column == picks[:, 2 * r + j : 2 * r + j + 1], 1.0, 0.0).astype(BF16)
            parts = []
            for half in range(2):
                g = 2 * j + half
                y_high, y_low = split(y[:, g * 128 : (g + 1) * 128])
                parts.append(jnp.where(first_half, y_high.astype(F32), y_low.astype(F32)).astype(BF16))
            term = jnp.dot(table, jnp.concatenate(parts, axis=0), preferred_element_type=F32)
            total = term if total is None else total + term
        total = total + pltpu.roll(total, BS, 1)
        coupled = jnp.where(first_half, total[:256], total[256:])
        spot = pl.ds(r, 256, stride=4)
        out_v[spot, :] = diag_v[spot, :] * x + coupled

    for peer in peers:
        cond_copy(peer, peer).wait_recv()
    for l in range(LEV):
        (face_copy() if l == LEV - 1 else pick_copy(l)).wait_send()
        idx_copy(l).wait_send()
        spread_copy(l).wait_send()
    for peer in peers:
        z_copy(rows_v, zrows_v, peer, z, peer, z_send, z_recv, peer).wait_send()
        cond_copy(peer, z).wait_send()


def last(part, cond, out_hbm, out_v, sem):
    copies = []
    for p in range(NZP):
        chunk = pl.ds(p * 128, 128)
        for r in range(4):
            spot = pl.ds(p * 128 + r, 32, stride=4)
            out_v[spot, :] = part[spot, :] - cond[pl.ds(p * 128 + r * 32, 32), :].astype(F32)
        copies.append(pltpu.make_async_copy(out_v.at[chunk], out_hbm.at[chunk], sem.at[p]))
        copies[-1].start()
    for copy in copies:
        copy.wait()


def local(sep_in, inv_blocks, couple_blocks, face_index, sep_diag, sep_couple, sep_index):
    sep_tiles = sep_in.reshape(4, 8, 32, 128).transpose(0, 2, 1, 3).reshape(1024, 128)
    diag_tiles = sep_diag.reshape(4, 256, 128).transpose(1, 0, 2).reshape(1024, 128)
    picks = sep_index.reshape(4, 512, 2).transpose(0, 2, 1)
    dma = pltpu.SemaphoreType.DMA
    part, cond = pl.pallas_call(
        kernel,
        out_shape=(pltpu.VMEM((1024, 128), F32), pltpu.VMEM((1024, 128), BF16)),
        in_specs=[pl.BlockSpec(memory_space=pl.ANY)] * 7,
        out_specs=(pl.BlockSpec(memory_space=pltpu.VMEM), pl.BlockSpec(memory_space=pltpu.VMEM)),
        scratch_shapes=[
            pltpu.VMEM((1024, 128), F32),
            pltpu.VMEM((64, 64, 128), BF16),
            pltpu.VMEM((2, 64, 64, 128), BF16),
            pltpu.VMEM((2, 128), jnp.int32),
            pltpu.VMEM((1024, 128), F32),
            pltpu.VMEM((2, 64, 64), F32),
            pltpu.VMEM((4, 2, 512), jnp.int32),
            pltpu.VMEM((1024, 128), F32),
            pltpu.VMEM((1024, 128), BF16),
            pltpu.VMEM((256, 128), BF16),
            pltpu.VMEM((1024, 128), F32),
            pltpu.VMEM((4, 2, 128), jnp.int32),
            pltpu.VMEM((3, 128, 128), BF16),
            pltpu.VMEM((3, 128, 128), BF16),
            pltpu.VMEM((128, 128), BF16),
            pltpu.VMEM((4, 128, 128), BF16),
            pltpu.VMEM((1024, 128), F32),
            pltpu.VMEM((1024, 128), BF16),
            pltpu.VMEM((64, 128), F32),
            pltpu.VMEM((64, 128), F32),
            pltpu.VMEM((512, 128), jnp.int32),
            dma((7,)),
            dma((4,)),
            dma((4,)),
            dma((4,)),
            dma((4,)),
            dma((8,)),
            dma((8,)),
            dma((4,)),
            dma((4,)),
            dma((8,)),
            dma((8,)),
        ],
        compiler_params=pltpu.CompilerParams(
            collective_id=0, has_side_effects=True, vmem_limit_bytes=62 * 1024 * 1024
        ),
        cost_estimate=pl.CostEstimate(flops=3_000_000_000, bytes_accessed=5_000_000, transcendentals=0),
    )(
        sep_tiles, inv_blocks.reshape(64, 64, 128), couple_blocks.reshape(2, 64, 64, 128),
        face_index.reshape(2, 128), diag_tiles, sep_couple, picks,
    )
    out = pl.pallas_call(
        last,
        out_shape=jax.ShapeDtypeStruct((1024, 128), F32),
        in_specs=[pl.BlockSpec(memory_space=pltpu.VMEM)] * 2,
        out_specs=pl.BlockSpec(memory_space=pl.ANY),
        scratch_shapes=[pltpu.VMEM((1024, 128), F32), dma((8,))],
    )(
        pltpu.with_memory_space_constraint(part, pltpu.VMEM),
        pltpu.with_memory_space_constraint(cond, pltpu.VMEM),
    )
    return out.reshape(256, 4, 128).transpose(1, 0, 2).reshape(1, 4, 32768)


def solution(mesh):
    return jax.shard_map(
        local,
        mesh=mesh,
        in_specs=(
            P("sub", None, None, "sep"),
            P("sub", None, None, "sep"),
            P("sub", None, None, None, "sep"),
            P("sub", None, "sep"),
            P("sub", "sep", None),
            P(),
            P("sub", "sep", None, None),
        ),
        out_specs=P("sub", "sep", None),
        check_vma=False,
    )
```

```python
import jax
import jax.numpy as jnp
from jax import lax
from jax.experimental import pallas as pl
from jax.experimental.pallas import tpu as pltpu
from jax.sharding import PartitionSpec as P

BS = 64
LEV = 4
NB = 128
NZP = 8
F32 = jnp.float32
BF16 = jnp.bfloat16
MESH = pl.DeviceIdType.MESH
TN = (((0,), (0,)), ((), ()))
NT = (((1,), (1,)), ((), ()))


def one_hot(rows, base, picks):
    place = lax.broadcasted_iota(jnp.int32, (rows, picks.shape[1]), 0) + base
    return jnp.where(place == picks, 1.0, 0.0).astype(BF16)


def halves_by_parity(values, odd):
    return jnp.concatenate([jnp.where(odd, 0.0, values), jnp.where(odd, values, 0.0)], axis=0)


def split(values):
    high = values.astype(BF16)
    return high, (values - high.astype(F32)).astype(BF16)


def kernel(
    sep_hbm, inv_hbm, couple_hbm, fidx_hbm, diag_hbm, w_hbm, sidx_hbm, out_v, cond_r,
    sep_v, inv_v, couple_v, fidx_v, diag_v, w_v, sidx_v,
    rows_v, face_v, far_v, zrows_v, fidx_r, pick_s, pick_r, spread_s, spread_r, cond_v, cond_s,
    driven_v, solved_v, sidx_t,
    in_sem, a_send, a_recv, i_send, i_recv, z_send, z_recv, c_send, c_recv, e_send, e_recv,
):
    s = lax.axis_index("sub")
    z = lax.axis_index("sep")
    side = [lax.rem(lax.div(s, 1 << l), 2) for l in range(LEV)]
    partner = [s + (1 - 2 * side[l]) * (1 << l) for l in range(LEV)]
    own_base = [pl.multiple_of(l * 512 + side[l] * 256, 256) for l in range(LEV)]
    far_base = (LEV - 1) * 512 + (1 - side[LEV - 1]) * 256
    peers = [lax.rem(z + d, NZP) for d in (4, 3, 5, 2, 6, 1, 7)]

    def local(i, src, dst):
        return pltpu.make_async_copy(src, dst, in_sem.at[i])

    loads = [
        local(0, sep_hbm, sep_v),
        local(1, fidx_hbm, fidx_v),
        local(2, couple_hbm, couple_v),
        local(3, inv_hbm, inv_v),
        local(4, sidx_hbm, sidx_v),
        local(5, w_hbm.at[lax.div(z, 2)], w_v),
        local(6, diag_hbm, diag_v),
    ]
    for load in loads:
        load.start()

    barrier = pltpu.get_barrier_semaphore()
    for l in range(LEV):
        pl.semaphore_signal(barrier, inc=1, device_id={"sub": partner[l]}, device_id_type=MESH)
    for peer in peers:
        pl.semaphore_signal(barrier, inc=1, device_id={"sep": peer}, device_id_type=MESH)

    loads[0].wait()
    for l in range(LEV):
        for c in range(8):
            row = sep_v[pl.ds(l * 256 + c, 32, stride=8), :]
            rows_v[pl.ds((l * 8 + c) * 32, 32), :] = row
            face_v[pl.ds((l * 8 + c) * 32, 32), :] = row.astype(BF16)
    loads[1].wait()

    pl.semaphore_wait(barrier, LEV + NZP - 1)

    def to_partner(l, src, dst, send, recv):
        return pltpu.make_async_remote_copy(
            src_ref=src, dst_ref=dst, send_sem=send.at[l], recv_sem=recv.at[l],
            device_id={"sub": partner[l]}, device_id_type=MESH,
        )

    def face_copy():
        return to_partner(LEV - 1, face_v.at[pl.ds((LEV - 1) * 256, 256)], far_v, a_send, a_recv)

    def pick_copy(l):
        return to_partner(l, pick_s.at[l], pick_r.at[l], a_send, a_recv)

    def idx_copy(l):
        return to_partner(l, fidx_v, fidx_r.at[l], i_send, i_recv)

    def spread_copy(l):
        return to_partner(l, spread_s, spread_r.at[l], c_send, c_recv)

    def z_copy(src, dst, slot, place, peer, send, recv, out_slot):
        return pltpu.make_async_remote_copy(
            src_ref=src.at[pl.ds(pl.multiple_of(out_slot * 128, 128), 128)],
            dst_ref=dst.at[pl.ds(pl.multiple_of(place * 128, 128), 128)],
            send_sem=send.at[slot], recv_sem=recv.at[place],
            device_id={"sep": peer}, device_id_type=MESH,
        )

    for l in (2, 1, 0):
        idx_copy(l).start()
    face_copy().start()
    idx_copy(LEV - 1).start()
    for peer in peers:
        z_copy(rows_v, zrows_v, peer, z, peer, z_send, z_recv, peer).start()
    mine = pl.ds(pl.multiple_of(z * 128, 128), 128)
    zrows_v[mine, :] = rows_v[mine, :]

    loads[4].wait()
    block = jnp.concatenate([sidx_v[r] for r in range(4)] * 16, axis=0)
    sidx_t[...] = jnp.transpose(lax.rem(block, 2) * 256 + lax.div(block, 2))

    def places(pair):
        both = jnp.concatenate([pair[0:1, :], pair[1:2, :]], axis=1)
        return lax.rem(both, 2) == 1, lax.div(both, 2)

    def picked_from(part, base, at):
        return lax.dot_general(part, one_hot(256, base, at), TN, preferred_element_type=F32)

    odd, place = places(fidx_v[...])
    picked = picked_from(face_v[pl.ds(0, 256), :], own_base[0], place)
    for l in range(1, LEV):
        picked += picked_from(face_v[pl.ds(l * 256, 256), :], own_base[l], place)
    loads[2].wait()
    loads[3].wait()
    for l in (0, 1, 2):
        idx_copy(l).wait_recv()
        got_odd, got_place = places(fidx_r[l])
        got = picked_from(face_v[pl.ds(l * 256, 256), :], own_base[l], got_place)
        got = jnp.where(got_odd, got[BS:], got[:BS])
        pick_s[l] = jnp.concatenate([got[:, :NB], got[:, NB:]], axis=0).astype(BF16)
        pick_copy(l).start()
    near = jnp.zeros((2 * BS, NB), F32)
    for l in (0, 1, 2):
        pick_copy(l).wait_recv()
        near += pick_r[l].astype(F32)
    face_copy().wait_recv()
    picked += picked_from(far_v[...], far_base, place)
    picked = jnp.where(odd, picked[BS:], picked[:BS])
    picked += jnp.concatenate([near[:BS], near[BS:]], axis=1)
    first, second = picked[:, :NB], picked[:, NB:]

    def rows_of(i, body):
        return jnp.concatenate([body(i * 8 + e) for e in range(8)], axis=0)

    def drive(i, carry):
        def one(row):
            total = couple_v[0, row].astype(F32) * first + couple_v[1, row].astype(F32) * second
            return jnp.sum(total, axis=0, keepdims=True)
        driven_v[pl.ds(pl.multiple_of(i * 8, 8), 8), :] = rows_of(i, one)
        return carry

    lax.fori_loop(0, 8, drive, 0, unroll=2)
    driven = driven_v[...].astype(BF16).astype(F32)

    def solve(i, carry):
        def one(row):
            return jnp.sum(inv_v[row].astype(F32) * driven, axis=0, keepdims=True)
        solved_v[pl.ds(pl.multiple_of(i * 8, 8), 8), :] = rows_of(i, one).astype(BF16).astype(F32)
        return carry

    lax.fori_loop(0, 8, solve, 0, unroll=2)

    def spread_step(i, carry):
        low, high = carry
        part = solved_v[pl.ds(pl.multiple_of(i * 8, 8), 8), :]
        for e in range(8):
            row = part[e : e + 1, :]
            low += couple_v[0, i * 8 + e].astype(F32) * row
            high += couple_v[1, i * 8 + e].astype(F32) * row
        return low, high

    zero = jnp.zeros((BS, NB), F32)
    low, high = lax.fori_loop(0, 8, spread_step, (zero, zero), unroll=2)
    spread_s[pl.ds(0, BS), :] = low.astype(BF16)
    spread_s[pl.ds(BS, BS), :] = high.astype(BF16)
    for l in (3, 2, 1, 0):
        spread_copy(l).start()

    own_high, own_low = split(halves_by_parity(jnp.concatenate([low, high], axis=1), odd))
    for l in range(LEV):
        table = one_hot(256, own_base[l], place)
        part = lax.dot_general(table, own_high, NT, preferred_element_type=F32)
        part += lax.dot_general(table, own_low, NT, preferred_element_type=F32)
        cond_v[pl.ds(l * 256, 256), :] = part

    def cond_copy(peer, place):
        return z_copy(cond_s, cond_r, peer, place, peer, e_send, e_recv, peer)

    for l in range(LEV):
        if l == LEV - 1:
            idx_copy(l).wait_recv()
        got_odd, got_place = places(fidx_r[l])
        spread_copy(l).wait_recv()
        values = spread_r[l].astype(F32)
        values = jnp.concatenate([values[:BS], values[BS:]], axis=1)
        values = halves_by_parity(values, got_odd).astype(BF16)
        table = one_hot(256, own_base[l], got_place)
        part = cond_v[pl.ds(l * 256, 256), :] + lax.dot_general(
            table, values, NT, preferred_element_type=F32
        )
        cond_s[pl.ds(l * 256, 256), :] = part.astype(BF16)
        for h in range(2):
            q = 2 * l + h

            @pl.when(z != q)
            def _():
                z_copy(cond_s, cond_r, q, z, q, e_send, e_recv, q).start()

            @pl.when(z == q)
            def _():
                cond_r[pl.ds(q * 128, 128), :] = cond_s[pl.ds(q * 128, 128), :]

    loads[5].wait()
    loads[6].wait()
    empty = jnp.zeros((BS, BS), F32)
    weights = []
    for j in range(2):
        w = w_v[j]
        left = jnp.concatenate([w, empty], axis=1)
        right = jnp.concatenate([empty, w], axis=1)
        weights += [left, left, right, right]
    w_high, w_low = split(jnp.concatenate(weights, axis=0))
    first_half = lax.broadcasted_iota(jnp.int32, (256, 128), 1) < BS
    column = lax.broadcasted_iota(jnp.int32, (512, 512), 1)
    picks = jnp.concatenate([sidx_t[pl.ds(e, 256, stride=2), :] for e in range(2)], axis=0)

    for peer in peers:
        z_copy(rows_v, zrows_v, peer, peer, peer, z_send, z_recv, peer).wait_recv()
    for r in range(4):
        x = jnp.concatenate([zrows_v[pl.ds(p * 128 + r * 32, 32), :] for p in range(NZP)], axis=0)
        x_high, x_low = split(x)
        y = lax.dot_general(x_high, w_high, NT, preferred_element_type=F32)
        y += lax.dot_general(x_low, w_high, NT, preferred_element_type=F32)
        y += lax.dot_general(x_high, w_low, NT, preferred_element_type=F32)
        total = None
        for j in range(2):
            table = jnp.where(column == picks[:, 2 * r + j : 2 * r + j + 1], 1.0, 0.0).astype(BF16)
            parts = []
            for half in range(2):
                g = 2 * j + half
                y_high, y_low = split(y[:, g * 128 : (g + 1) * 128])
                parts.append(jnp.where(first_half, y_high.astype(F32), y_low.astype(F32)).astype(BF16))
            term = jnp.dot(table, jnp.concatenate(parts, axis=0), preferred_element_type=F32)
            total = term if total is None else total + term
        total = total + pltpu.roll(total, BS, 1)
        coupled = jnp.where(first_half, total[:256], total[256:])
        spot = pl.ds(r, 256, stride=4)
        out_v[spot, :] = diag_v[spot, :] * x + coupled

    for peer in peers:
        cond_copy(peer, peer).wait_recv()
    for l in range(LEV):
        (face_copy() if l == LEV - 1 else pick_copy(l)).wait_send()
        idx_copy(l).wait_send()
        spread_copy(l).wait_send()
    for peer in peers:
        z_copy(rows_v, zrows_v, peer, z, peer, z_send, z_recv, peer).wait_send()
        cond_copy(peer, z).wait_send()


def last(part, cond, out_hbm, out_v, sem):
    copies = []
    for p in range(NZP):
        chunk = pl.ds(p * 128, 128)
        for r in range(4):
            spot = pl.ds(p * 128 + r, 32, stride=4)
            out_v[spot, :] = part[spot, :] - cond[pl.ds(p * 128 + r * 32, 32), :].astype(F32)
        copies.append(pltpu.make_async_copy(out_v.at[chunk], out_hbm.at[chunk], sem.at[p]))
        copies[-1].start()
    for copy in copies:
        copy.wait()


def local(sep_in, inv_blocks, couple_blocks, face_index, sep_diag, sep_couple, sep_index):
    sep_tiles = sep_in.reshape(4, 8, 32, 128).transpose(0, 2, 1, 3).reshape(1024, 128)
    diag_tiles = sep_diag.reshape(4, 256, 128).transpose(1, 0, 2).reshape(1024, 128)
    picks = sep_index.reshape(4, 512, 2).transpose(0, 2, 1)
    dma = pltpu.SemaphoreType.DMA
    part, cond = pl.pallas_call(
        kernel,
        out_shape=(pltpu.VMEM((1024, 128), F32), pltpu.VMEM((1024, 128), BF16)),
        in_specs=[pl.BlockSpec(memory_space=pl.ANY)] * 7,
        out_specs=(pl.BlockSpec(memory_space=pltpu.VMEM), pl.BlockSpec(memory_space=pltpu.VMEM)),
        scratch_shapes=[
            pltpu.VMEM((1024, 128), F32),
            pltpu.VMEM((64, 64, 128), BF16),
            pltpu.VMEM((2, 64, 64, 128), BF16),
            pltpu.VMEM((2, 128), jnp.int32),
            pltpu.VMEM((1024, 128), F32),
            pltpu.VMEM((2, 64, 64), F32),
            pltpu.VMEM((4, 2, 512), jnp.int32),
            pltpu.VMEM((1024, 128), F32),
            pltpu.VMEM((1024, 128), BF16),
            pltpu.VMEM((256, 128), BF16),
            pltpu.VMEM((1024, 128), F32),
            pltpu.VMEM((4, 2, 128), jnp.int32),
            pltpu.VMEM((3, 128, 128), BF16),
            pltpu.VMEM((3, 128, 128), BF16),
            pltpu.VMEM((128, 128), BF16),
            pltpu.VMEM((4, 128, 128), BF16),
            pltpu.VMEM((1024, 128), F32),
            pltpu.VMEM((1024, 128), BF16),
            pltpu.VMEM((64, 128), F32),
            pltpu.VMEM((64, 128), F32),
            pltpu.VMEM((512, 128), jnp.int32),
            dma((7,)),
            dma((4,)),
            dma((4,)),
            dma((4,)),
            dma((4,)),
            dma((8,)),
            dma((8,)),
            dma((4,)),
            dma((4,)),
            dma((8,)),
            dma((8,)),
        ],
        compiler_params=pltpu.CompilerParams(
            collective_id=0, has_side_effects=True, vmem_limit_bytes=62 * 1024 * 1024
        ),
        cost_estimate=pl.CostEstimate(flops=3_000_000_000, bytes_accessed=5_000_000, transcendentals=0),
    )(
        sep_tiles, inv_blocks.reshape(64, 64, 128), couple_blocks.reshape(2, 64, 64, 128),
        face_index.reshape(2, 128), diag_tiles, sep_couple, picks,
    )
    out = pl.pallas_call(
        last,
        out_shape=jax.ShapeDtypeStruct((1024, 128), F32),
        in_specs=[pl.BlockSpec(memory_space=pltpu.VMEM)] * 2,
        out_specs=pl.BlockSpec(memory_space=pl.ANY),
        scratch_shapes=[pltpu.VMEM((1024, 128), F32), dma((8,))],
    )(
        pltpu.with_memory_space_constraint(part, pltpu.VMEM),
        pltpu.with_memory_space_constraint(cond, pltpu.VMEM),
    )
    return out.reshape(256, 4, 128).transpose(1, 0, 2).reshape(1, 4, 32768)


def solution(mesh):
    return jax.shard_map(
        local,
        mesh=mesh,
        in_specs=(
            P("sub", None, None, "sep"),
            P("sub", None, None, "sep"),
            P("sub", None, None, None, "sep"),
            P("sub", None, "sep"),
            P("sub", "sep", None),
            P(),
            P("sub", "sep", None, None),
        ),
        out_specs=P("sub", "sep", None),
        check_vma=False,
    )
```

```python
import jax
import jax.numpy as jnp
from jax import lax
from jax.experimental import pallas as pl
from jax.experimental.pallas import tpu as pltpu
from jax.sharding import PartitionSpec as P

BS = 64
LEV = 4
NB = 128
NZP = 8
F32 = jnp.float32
BF16 = jnp.bfloat16
MESH = pl.DeviceIdType.MESH
TN = (((0,), (0,)), ((), ()))
NT = (((1,), (1,)), ((), ()))


def one_hot(rows, base, picks):
    place = lax.broadcasted_iota(jnp.int32, (rows, picks.shape[1]), 0) + base
    return jnp.where(place == picks, 1.0, 0.0).astype(BF16)


def halves_by_parity(values, odd):
    return jnp.concatenate([jnp.where(odd, 0.0, values), jnp.where(odd, values, 0.0)], axis=0)


def split(values):
    high = values.astype(BF16)
    return high, (values - high.astype(F32)).astype(BF16)


def kernel(
    sep_hbm, inv_hbm, couple_hbm, fidx_hbm, diag_hbm, w_hbm, sidx_hbm, out_v, cond_r,
    sep_v, inv_v, couple_v, fidx_v, diag_v, w_v, sidx_v,
    rows_v, face_v, turned_v, far_v, tables_v, zrows_v, fidx_r, pick_s, pick_r, spread_s, spread_r, cond_v, cond_s,
    driven_v, solved_v, sidx_t, hot_v,
    in_sem, a_send, a_recv, i_send, i_recv, z_send, z_recv, c_send, c_recv, e_send, e_recv,
):
    s = lax.axis_index("sub")
    z = lax.axis_index("sep")
    side = [lax.rem(lax.div(s, 1 << l), 2) for l in range(LEV)]
    partner = [s + (1 - 2 * side[l]) * (1 << l) for l in range(LEV)]
    own_base = [pl.multiple_of(l * 512 + side[l] * 256, 256) for l in range(LEV)]
    far_base = (LEV - 1) * 512 + (1 - side[LEV - 1]) * 256
    peers = [lax.rem(z + d, NZP) for d in (4, 3, 5, 2, 6, 1, 7)]

    def local(i, src, dst):
        return pltpu.make_async_copy(src, dst, in_sem.at[i])

    loads = [
        local(0, sep_hbm, sep_v),
        local(1, fidx_hbm, fidx_v),
        local(2, couple_hbm, couple_v),
        local(3, inv_hbm, inv_v),
        local(4, sidx_hbm, sidx_v),
        local(5, w_hbm.at[lax.div(z, 2)], w_v),
        local(6, diag_hbm, diag_v),
    ]
    for load in loads:
        load.start()

    barrier = pltpu.get_barrier_semaphore()
    for l in range(LEV):
        pl.semaphore_signal(barrier, inc=1, device_id={"sub": partner[l]}, device_id_type=MESH)
    for peer in peers:
        pl.semaphore_signal(barrier, inc=1, device_id={"sep": peer}, device_id_type=MESH)

    loads[0].wait()
    for l in range(LEV):
        for c in range(8):
            row = sep_v[pl.ds(l * 256 + c, 32, stride=8), :]
            rows_v[pl.ds((l * 8 + c) * 32, 32), :] = row
            face_v[pl.ds((l * 8 + c) * 32, 32), :] = row.astype(BF16)
    turned_v[...] = jnp.transpose(rows_v[pl.ds((LEV - 1) * 256, 256), :]).astype(BF16)
    loads[1].wait()

    pl.semaphore_wait(barrier, LEV + NZP - 1)

    def to_partner(l, src, dst, send, recv):
        return pltpu.make_async_remote_copy(
            src_ref=src, dst_ref=dst, send_sem=send.at[l], recv_sem=recv.at[l],
            device_id={"sub": partner[l]}, device_id_type=MESH,
        )

    def face_copy():
        return to_partner(LEV - 1, turned_v, far_v, a_send, a_recv)

    def pick_copy(l):
        return to_partner(l, pick_s.at[l], pick_r.at[l], a_send, a_recv)

    def idx_copy(l):
        return to_partner(l, fidx_v, fidx_r.at[l], i_send, i_recv)

    def spread_copy(l):
        return to_partner(l, spread_s, spread_r.at[l], c_send, c_recv)

    def z_copy(src, dst, slot, place, peer, send, recv, out_slot):
        return pltpu.make_async_remote_copy(
            src_ref=src.at[pl.ds(pl.multiple_of(out_slot * 128, 128), 128)],
            dst_ref=dst.at[pl.ds(pl.multiple_of(place * 128, 128), 128)],
            send_sem=send.at[slot], recv_sem=recv.at[place],
            device_id={"sep": peer}, device_id_type=MESH,
        )

    for l in (2, 1, 0):
        idx_copy(l).start()
    face_copy().start()
    idx_copy(LEV - 1).start()
    for peer in peers:
        z_copy(rows_v, zrows_v, peer, z, peer, z_send, z_recv, peer).start()
    mine = pl.ds(pl.multiple_of(z * 128, 128), 128)
    zrows_v[mine, :] = rows_v[mine, :]

    loads[4].wait()
    block = jnp.concatenate([sidx_v[r] for r in range(4)] * 16, axis=0)
    sidx_t[...] = jnp.transpose(lax.rem(block, 2) * 256 + lax.div(block, 2))

    def places(pair):
        both = jnp.concatenate([pair[0:1, :], pair[1:2, :]], axis=1)
        return lax.rem(both, 2) == 1, lax.div(both, 2)

    def picked_from(part, base, at):
        return lax.dot_general(part, one_hot(256, base, at), TN, preferred_element_type=F32)

    odd, place = places(fidx_v[...])
    picked = picked_from(face_v[pl.ds(0, 256), :], own_base[0], place)
    for l in range(1, LEV):
        picked += picked_from(face_v[pl.ds(l * 256, 256), :], own_base[l], place)
    picked = jnp.where(odd, picked[BS:], picked[:BS])
    tables_v[0] = one_hot(256, far_base, place)
    loads[2].wait()
    loads[3].wait()
    for l in (0, 1, 2):
        idx_copy(l).wait_recv()
        got_odd, got_place = places(fidx_r[l])
        got = picked_from(face_v[pl.ds(l * 256, 256), :], own_base[l], got_place)
        got = jnp.where(got_odd, got[BS:], got[:BS])
        pick_s[l] = jnp.concatenate([got[:, :NB], got[:, NB:]], axis=0).astype(BF16)
        pick_copy(l).start()
    column = lax.broadcasted_iota(jnp.int32, (512, 512), 1)
    picks = jnp.concatenate([sidx_t[pl.ds(e, 256, stride=2), :] for e in range(2)], axis=0)
    for g in range(8):
        hot_v[g] = jnp.where(column == picks[:, g : g + 1], 1.0, 0.0).astype(BF16)
    near = jnp.zeros((2 * BS, NB), F32)
    for l in (0, 1, 2):
        pick_copy(l).wait_recv()
        near += pick_r[l].astype(F32)
    picked += jnp.concatenate([near[:BS], near[BS:]], axis=1)
    face_copy().wait_recv()
    far = jnp.dot(far_v[...], tables_v[0], preferred_element_type=F32)
    picked += jnp.where(odd, far[BS:], far[:BS])
    first, second = picked[:, :NB], picked[:, NB:]

    def rows_of(i, body):
        return jnp.concatenate([body(i * 8 + e) for e in range(8)], axis=0)

    def drive(i, carry):
        def one(row):
            total = couple_v[0, row].astype(F32) * first + couple_v[1, row].astype(F32) * second
            return jnp.sum(total, axis=0, keepdims=True)
        driven_v[pl.ds(pl.multiple_of(i * 8, 8), 8), :] = rows_of(i, one)
        return carry

    lax.fori_loop(0, 8, drive, 0, unroll=2)
    driven = driven_v[...].astype(BF16).astype(F32)

    def solve(i, carry):
        def one(row):
            return jnp.sum(inv_v[row].astype(F32) * driven, axis=0, keepdims=True)
        solved_v[pl.ds(pl.multiple_of(i * 8, 8), 8), :] = rows_of(i, one).astype(BF16).astype(F32)
        return carry

    lax.fori_loop(0, 8, solve, 0, unroll=2)

    def spread_step(i, carry):
        low, high = carry
        part = solved_v[pl.ds(pl.multiple_of(i * 8, 8), 8), :]
        for e in range(8):
            row = part[e : e + 1, :]
            low += couple_v[0, i * 8 + e].astype(F32) * row
            high += couple_v[1, i * 8 + e].astype(F32) * row
        return low, high

    zero = jnp.zeros((BS, NB), F32)
    low, high = lax.fori_loop(0, 8, spread_step, (zero, zero), unroll=2)
    spread_s[pl.ds(0, BS), :] = low.astype(BF16)
    spread_s[pl.ds(BS, BS), :] = high.astype(BF16)
    for l in (3, 2, 1, 0):
        spread_copy(l).start()

    own_high, own_low = split(halves_by_parity(jnp.concatenate([low, high], axis=1), odd))
    for l in range(LEV):
        table = one_hot(256, own_base[l], place)
        part = lax.dot_general(table, own_high, NT, preferred_element_type=F32)
        part += lax.dot_general(table, own_low, NT, preferred_element_type=F32)
        cond_v[pl.ds(l * 256, 256), :] = part

    def cond_copy(peer, place):
        return z_copy(cond_s, cond_r, peer, place, peer, e_send, e_recv, peer)

    for l in range(LEV):
        if l == LEV - 1:
            idx_copy(l).wait_recv()
        got_odd, got_place = places(fidx_r[l])
        if l == LEV - 1:
            tables_v[1] = one_hot(256, own_base[l], got_place)
        spread_copy(l).wait_recv()
        values = spread_r[l].astype(F32)
        values = jnp.concatenate([values[:BS], values[BS:]], axis=1)
        values = halves_by_parity(values, got_odd).astype(BF16)
        table = tables_v[1] if l == LEV - 1 else one_hot(256, own_base[l], got_place)
        part = cond_v[pl.ds(l * 256, 256), :] + lax.dot_general(
            table, values, NT, preferred_element_type=F32
        )
        cond_s[pl.ds(l * 256, 256), :] = part.astype(BF16)
        for h in range(2):
            q = 2 * l + h

            @pl.when(z != q)
            def _():
                z_copy(cond_s, cond_r, q, z, q, e_send, e_recv, q).start()

            @pl.when(z == q)
            def _():
                cond_r[pl.ds(q * 128, 128), :] = cond_s[pl.ds(q * 128, 128), :]

    loads[5].wait()
    loads[6].wait()
    empty = jnp.zeros((BS, BS), F32)
    weights = []
    for j in range(2):
        w = w_v[j]
        left = jnp.concatenate([w, empty], axis=1)
        right = jnp.concatenate([empty, w], axis=1)
        weights += [left, left, right, right]
    w_high, w_low = split(jnp.concatenate(weights, axis=0))
    first_half = lax.broadcasted_iota(jnp.int32, (256, 128), 1) < BS

    for peer in peers:
        z_copy(rows_v, zrows_v, peer, peer, peer, z_send, z_recv, peer).wait_recv()
    for r in range(4):
        x = jnp.concatenate([zrows_v[pl.ds(p * 128 + r * 32, 32), :] for p in range(NZP)], axis=0)
        x_high, x_low = split(x)
        y = lax.dot_general(x_high, w_high, NT, preferred_element_type=F32)
        y += lax.dot_general(x_low, w_high, NT, preferred_element_type=F32)
        y += lax.dot_general(x_high, w_low, NT, preferred_element_type=F32)
        total = None
        for j in range(2):
            table = hot_v[2 * r + j]
            parts = []
            for half in range(2):
                g = 2 * j + half
                y_high, y_low = split(y[:, g * 128 : (g + 1) * 128])
                parts.append(jnp.where(first_half, y_high.astype(F32), y_low.astype(F32)).astype(BF16))
            term = jnp.dot(table, jnp.concatenate(parts, axis=0), preferred_element_type=F32)
            total = term if total is None else total + term
        total = total + pltpu.roll(total, BS, 1)
        coupled = jnp.where(first_half, total[:256], total[256:])
        spot = pl.ds(r, 256, stride=4)
        out_v[spot, :] = diag_v[spot, :] * x + coupled

    for peer in peers:
        cond_copy(peer, peer).wait_recv()
    for l in range(LEV):
        (face_copy() if l == LEV - 1 else pick_copy(l)).wait_send()
        idx_copy(l).wait_send()
        spread_copy(l).wait_send()
    for peer in peers:
        z_copy(rows_v, zrows_v, peer, z, peer, z_send, z_recv, peer).wait_send()
        cond_copy(peer, z).wait_send()


def last(part, cond, out_hbm, out_v, sem):
    copies = []
    for p in range(NZP):
        chunk = pl.ds(p * 128, 128)
        for r in range(4):
            spot = pl.ds(p * 128 + r, 32, stride=4)
            out_v[spot, :] = part[spot, :] - cond[pl.ds(p * 128 + r * 32, 32), :].astype(F32)
        copies.append(pltpu.make_async_copy(out_v.at[chunk], out_hbm.at[chunk], sem.at[p]))
        copies[-1].start()
    for copy in copies:
        copy.wait()


def local(sep_in, inv_blocks, couple_blocks, face_index, sep_diag, sep_couple, sep_index):
    sep_tiles = sep_in.reshape(4, 8, 32, 128).transpose(0, 2, 1, 3).reshape(1024, 128)
    diag_tiles = sep_diag.reshape(4, 256, 128).transpose(1, 0, 2).reshape(1024, 128)
    picks = sep_index.reshape(4, 512, 2).transpose(0, 2, 1)
    dma = pltpu.SemaphoreType.DMA
    part, cond = pl.pallas_call(
        kernel,
        out_shape=(pltpu.VMEM((1024, 128), F32), pltpu.VMEM((1024, 128), BF16)),
        in_specs=[pl.BlockSpec(memory_space=pl.ANY)] * 7,
        out_specs=(pl.BlockSpec(memory_space=pltpu.VMEM), pl.BlockSpec(memory_space=pltpu.VMEM)),
        scratch_shapes=[
            pltpu.VMEM((1024, 128), F32),
            pltpu.VMEM((64, 64, 128), BF16),
            pltpu.VMEM((2, 64, 64, 128), BF16),
            pltpu.VMEM((2, 128), jnp.int32),
            pltpu.VMEM((1024, 128), F32),
            pltpu.VMEM((2, 64, 64), F32),
            pltpu.VMEM((4, 2, 512), jnp.int32),
            pltpu.VMEM((1024, 128), F32),
            pltpu.VMEM((1024, 128), BF16),
            pltpu.VMEM((128, 256), BF16),
            pltpu.VMEM((128, 256), BF16),
            pltpu.VMEM((2, 256, 256), BF16),
            pltpu.VMEM((1024, 128), F32),
            pltpu.VMEM((4, 2, 128), jnp.int32),
            pltpu.VMEM((3, 128, 128), BF16),
            pltpu.VMEM((3, 128, 128), BF16),
            pltpu.VMEM((128, 128), BF16),
            pltpu.VMEM((4, 128, 128), BF16),
            pltpu.VMEM((1024, 128), F32),
            pltpu.VMEM((1024, 128), BF16),
            pltpu.VMEM((64, 128), F32),
            pltpu.VMEM((64, 128), F32),
            pltpu.VMEM((512, 128), jnp.int32),
            pltpu.VMEM((8, 512, 512), BF16),
            dma((7,)),
            dma((4,)),
            dma((4,)),
            dma((4,)),
            dma((4,)),
            dma((8,)),
            dma((8,)),
            dma((4,)),
            dma((4,)),
            dma((8,)),
            dma((8,)),
        ],
        compiler_params=pltpu.CompilerParams(
            collective_id=0, has_side_effects=True, vmem_limit_bytes=62 * 1024 * 1024
        ),
        cost_estimate=pl.CostEstimate(flops=3_000_000_000, bytes_accessed=5_000_000, transcendentals=0),
    )(
        sep_tiles, inv_blocks.reshape(64, 64, 128), couple_blocks.reshape(2, 64, 64, 128),
        face_index.reshape(2, 128), diag_tiles, sep_couple, picks,
    )
    out = pl.pallas_call(
        last,
        out_shape=jax.ShapeDtypeStruct((1024, 128), F32),
        in_specs=[pl.BlockSpec(memory_space=pltpu.VMEM)] * 2,
        out_specs=pl.BlockSpec(memory_space=pl.ANY),
        scratch_shapes=[pltpu.VMEM((1024, 128), F32), dma((8,))],
    )(
        pltpu.with_memory_space_constraint(part, pltpu.VMEM),
        pltpu.with_memory_space_constraint(cond, pltpu.VMEM),
    )
    return out.reshape(256, 4, 128).transpose(1, 0, 2).reshape(1, 4, 32768)


def solution(mesh):
    return jax.shard_map(
        local,
        mesh=mesh,
        in_specs=(
            P("sub", None, None, "sep"),
            P("sub", None, None, "sep"),
            P("sub", None, None, None, "sep"),
            P("sub", None, "sep"),
            P("sub", "sep", None),
            P(),
            P("sub", "sep", None, None),
        ),
        out_specs=P("sub", "sep", None),
        check_vma=False,
    )
```
